32 devices in a mesh: dp: 4 (over z), ctx: 8 (over y, x, core).
Axes of the slice: x: 2, y: 2, z: 4, core: 2. Of those that a mesh axis runs over, the one named last changes fastest.
Arguments:
- query_input: bfloat16 [4, 1024, 8192], P('dp', 'ctx'), may hold values from -12 to 12
- key_input: bfloat16 [4, 1024, 1024], P('dp', 'ctx'), may hold values from -12 to 12
- value_input: bfloat16 [4, 1024, 1024], P('dp', 'ctx'), may hold values from -6 to 6
- out_grad: bfloat16 [4, 1024, 8192], P('dp', 'ctx'), may hold values from -6 to 6
- query_bias: float32 [8192], replicated, may hold values from -1.75 to 1.75
- key_bias: float32 [1024], replicated, may hold values from -1.75 to 1.75
- value_bias: float32 [1024], replicated, may hold values from -1.75 to 1.75
- parents: int32 [4, 8], P('dp'), may hold values from 0 to 6, as said below
Outputs:
- attended: bfloat16 [4, 1024, 8192], P('dp', 'ctx')
- query_grad: float32 [4, 1024, 8192], P('dp', 'ctx')
- key_grad: float32 [4, 1024, 1024], P('dp', 'ctx')
- value_grad: float32 [4, 1024, 1024], P('dp', 'ctx')
- query_bias_grad: float32 [8192], replicated
- key_bias_grad: float32 [1024], replicated
- value_bias_grad: float32 [1024], replicated
The draws below stay inside these ranges and needn't reach their ends.
Inputs may be any that keep to these rules, and one draw needn't show every extreme that they name: parents[t, 0] = 0 marks the root block; every other block's parent is an earlier block; the last block's parent is the block before it.
All inputs are finite; a program needn't handle non-finite values.
Results may differ from the reference program's by a relative error of at most 0.028.
Values may be sent and summed in bfloat16 or wider, within the bound.
A program may use at most 128 MiB of HBM per device.

```python
import math
import jax
import jax.numpy as jnp
from jax import lax

Q_HEADS = 64
KV_HEADS = 8
HEAD = 128
BLOCK = 128
TREES = 4
TREE_BLOCKS = 8
TREE_LEN = 1024
Q_WIDTH = 8192
KV_WIDTH = 1024


def draw_query_input(key, part):
    return jnp.clip(jax.random.normal(jax.random.fold_in(key, 1), (TREES, TREE_LEN, Q_HEADS * HEAD), jnp.float32) * 1.4, -8.0, 8.0).astype(jnp.bfloat16)


def draw_key_input(key, part):
    return jnp.clip(jax.random.normal(jax.random.fold_in(key, 2), (TREES, TREE_LEN, KV_HEADS * HEAD), jnp.float32) * 1.4, -8.0, 8.0).astype(jnp.bfloat16)


def draw_parents(key, part):
    block_ids = jnp.broadcast_to(jnp.arange(TREE_BLOCKS, dtype=jnp.int32), (TREES, TREE_BLOCKS))
    coin_flips = jax.random.randint(jax.random.fold_in(key, 29), (TREES, TREE_BLOCKS), 0, 2)
    picked = jax.random.randint(jax.random.fold_in(key, 31), (TREES, TREE_BLOCKS), 0, jnp.maximum(block_ids, 1))
    chosen = jnp.where(coin_flips == 1, block_ids - 1, picked)
    chosen = jnp.where(block_ids == 0, 0, chosen)
    chosen = jnp.where(block_ids == TREE_BLOCKS - 1, TREE_BLOCKS - 2, chosen)
    return chosen.astype(jnp.int32)


def level_of(key, dims, pieces, smallest, largest):
    factor_of, own = 1.0, jax.random.fold_in(key, 6)
    for position, parts in pieces:
        steps = jnp.exp(jax.random.uniform(jax.random.fold_in(own, position), (parts,), jnp.float32, smallest / len(pieces), largest / len(pieces)))
        factor_of = factor_of * jnp.repeat(steps, dims[position] // parts).reshape([-1 if axis == position else 1 for axis in range(len(dims))])
    return factor_of


def gaussian(key, dims, deviation, most, split=(), kind=jnp.bfloat16):
    values = deviation * jax.random.normal(key, dims, jnp.float32)
    if split:
        values = values * level_of(key, dims, split, -0.22, 0.18)
    return jnp.clip(values, -most, most).astype(kind)


def setup_inputs(seed: int = 0) -> dict:
    streams_of = jax.random.split(jax.random.key(seed), 9)
    query_input = draw_query_input(jax.random.fold_in(streams_of[8], 71), 0)
    key_input = draw_key_input(jax.random.fold_in(streams_of[8], 71), 0)
    value_input = gaussian(streams_of[2], (TREES, TREE_LEN, KV_WIDTH), 1.0, 6.0, ((0, 4), (1, 8)))
    out_grad = gaussian(streams_of[3], (TREES, TREE_LEN, Q_WIDTH), 1.0, 6.0, ((0, 4), (1, 8)))
    query_bias = gaussian(streams_of[4], (Q_WIDTH,), 0.3, 1.75, (), jnp.float32)
    key_bias = gaussian(streams_of[5], (KV_WIDTH,), 0.3, 1.75, (), jnp.float32)
    value_bias = gaussian(streams_of[6], (KV_WIDTH,), 0.3, 1.75, (), jnp.float32)
    parents = draw_parents(jax.random.fold_in(streams_of[8], 71), 0)
    return {"query_input": query_input, "key_input": key_input, "value_input": value_input, "out_grad": out_grad, "query_bias": query_bias, "key_bias": key_bias, "value_bias": value_bias, "parents": parents}


LOG_BASE = math.log(1000000.0)
NEG_LARGE = -1e30


def ancestry(parent_list):
    block_count = parent_list.shape[0]
    block_ids = jnp.arange(block_count, dtype=jnp.int32)
    step_matrix = ((parent_list[:, None] == block_ids[None, :]) & (block_ids[:, None] > 0)).astype(jnp.float32)
    identity = jnp.eye(block_count, dtype=jnp.float32)

    def advance(iteration, current):
        return identity + jnp.dot(step_matrix, current, precision=lax.Precision.HIGHEST)

    return lax.fori_loop(0, block_count, advance, identity)


def rotate(values, places, direction):
    half_width = values.shape[-1] // 2
    frequency = jnp.exp(jnp.arange(half_width, dtype=jnp.float32) * (-2.0 * LOG_BASE / values.shape[-1]))
    angles = places[..., None] * frequency
    cosine = jnp.cos(angles)[..., None, :]
    sine_part = direction * jnp.sin(angles)[..., None, :]
    first_half = values[..., :half_width]
    second = values[..., half_width:]
    return jnp.concatenate([first_half * cosine - second * sine_part, second * cosine + first_half * sine_part], axis=-1)


def rounded(values):
    return lax.optimization_barrier(values.astype(jnp.bfloat16)).astype(jnp.float32)


def reference(query_input, key_input, value_input, out_grad, query_bias, key_bias, value_bias, parents):
    score_scale = HEAD ** -0.5
    group_size = Q_HEADS // KV_HEADS

    def one_tree(tree_items):
        query_tree, key_tree, value_tree, grad_tree, parent_list = tree_items
        ancestors = ancestry(parent_list)
        block_depth = jnp.sum(ancestors, axis=1) - 1.0
        offsets = jnp.arange(BLOCK, dtype=jnp.float32)
        places = (block_depth[:, None] * BLOCK + offsets[None, :]).reshape(TREE_LEN)
        queries = rotate((query_tree.astype(jnp.float32) + query_bias).reshape(TREE_LEN, Q_HEADS, HEAD), places, 1.0).astype(jnp.bfloat16)
        key_rows = rotate((key_tree.astype(jnp.float32) + key_bias).reshape(TREE_LEN, KV_HEADS, HEAD), places, 1.0).astype(jnp.bfloat16)
        value_rows = (value_tree.astype(jnp.float32) + value_bias).astype(jnp.bfloat16).reshape(TREE_LEN, KV_HEADS, HEAD)
        queries = queries.reshape(TREE_LEN, KV_HEADS, group_size, HEAD)
        grad_rows = grad_tree.reshape(TREE_LEN, KV_HEADS, group_size, HEAD)
        key_float = key_rows.astype(jnp.float32)
        value_float = value_rows.astype(jnp.float32)
        token_block = jnp.arange(TREE_LEN, dtype=jnp.int32) // BLOCK
        token_offset = jnp.arange(TREE_LEN, dtype=jnp.int32) % BLOCK
        row_offset = jnp.arange(BLOCK, dtype=jnp.int32)

        def per_block(carried, query_block):
            key_acc, value_acc, query_total = carried
            first_row = query_block * BLOCK
            query_tile = lax.dynamic_slice_in_dim(queries, first_row, BLOCK, 0).astype(jnp.float32)
            grad_tile = lax.dynamic_slice_in_dim(grad_rows, first_row, BLOCK, 0).astype(jnp.float32)
            reach_row = lax.dynamic_index_in_dim(ancestors, query_block, 0, keepdims=False)[token_block] > 0.5
            causal = (token_block[None, :] != query_block) | (token_offset[None, :] <= row_offset[:, None])
            tile_mask = (reach_row[None, :] & causal)[:, None, None, :]
            scores = jnp.einsum('qghd,kgd->qghk', query_tile, key_float) * score_scale
            scores = jnp.where(tile_mask, scores, NEG_LARGE)
            row_peak = jnp.max(scores, axis=-1)
            weights = jnp.where(tile_mask, jnp.exp(scores - row_peak[..., None]), 0.0)
            total_sum = jnp.sum(weights, axis=-1)
            mixed_sum = jnp.einsum('qghk,kgd->qghd', rounded(weights), value_float)
            out_tile = (mixed_sum / total_sum[..., None]).astype(jnp.bfloat16)
            log_total = row_peak + jnp.log(total_sum)
            row_delta = jnp.sum(grad_tile * out_tile.astype(jnp.float32), axis=-1)
            probabilities = jnp.where(tile_mask, jnp.exp(scores - log_total[..., None]), 0.0)
            grad_probs = jnp.einsum('qghd,kgd->qghk', grad_tile, value_float)
            grad_scores = probabilities * (grad_probs - row_delta[..., None])
            grad_low = rounded(grad_scores)
            query_rot = jnp.einsum('qghk,kgd->qghd', grad_low, key_float) * score_scale
            key_acc = key_acc + jnp.einsum('qghk,qghd->kgd', grad_low, query_tile) * score_scale
            value_acc = value_acc + jnp.einsum('qghk,qghd->kgd', rounded(probabilities), grad_tile)
            row_places = lax.dynamic_slice_in_dim(places, first_row, BLOCK, 0)
            query_full = rotate(query_rot.reshape(BLOCK, Q_HEADS, HEAD), row_places, -1.0).reshape(BLOCK, Q_WIDTH)
            return (key_acc, value_acc, query_total + jnp.sum(query_full, axis=0)), (out_tile.reshape(BLOCK, Q_WIDTH), query_full)

        start_carry = (jnp.zeros((TREE_LEN, KV_HEADS, HEAD), jnp.float32), jnp.zeros((TREE_LEN, KV_HEADS, HEAD), jnp.float32), jnp.zeros((Q_WIDTH,), jnp.float32))
        (key_acc, value_acc, query_total), (out_rows, query_rows) = lax.scan(per_block, start_carry, jnp.arange(TREE_BLOCKS, dtype=jnp.int32))
        key_full = rotate(key_acc, places, -1.0).reshape(TREE_LEN, KV_WIDTH)
        value_full = value_acc.reshape(TREE_LEN, KV_WIDTH)
        return (out_rows.reshape(TREE_LEN, Q_WIDTH), query_rows.reshape(TREE_LEN, Q_WIDTH), key_full, value_full, query_total, jnp.sum(key_full, axis=0), jnp.sum(value_full, axis=0))

    results = lax.map(one_tree, (query_input, key_input, value_input, out_grad, parents))
    return (results[0], results[1], results[2], results[3], jnp.sum(results[4], axis=0), jnp.sum(results[5], axis=0), jnp.sum(results[6], axis=0))
```

```python
import functools
import math

import jax
import jax.numpy as jnp
import numpy as np
from jax import lax
from jax.experimental import pallas as pl
from jax.experimental.pallas import tpu as pltpu
from jax.sharding import PartitionSpec as P

Q_HEADS = 64
KV_HEADS = 8
HEAD = 128
GROUP = Q_HEADS // KV_HEADS
HALF = HEAD // 2
NEG_LARGE = -1e30
SCALE = HEAD ** (-0.5)
LOG2_SCALE = SCALE * math.log2(math.e)
LN2 = math.log(2.0)
MESH = pl.DeviceIdType.MESH


def tables(depths, rows):
    frequency = 1000000.0 ** (-2.0 * np.arange(HALF) / HEAD)
    places = (np.arange(depths)[:, None] * rows + np.arange(rows)[None, :]).astype(np.float64)
    angles = places[..., None] * frequency
    cosine, sine = np.cos(angles), np.sin(angles)
    flat = np.stack(
        [np.concatenate([cosine, cosine], -1), np.concatenate([-sine, sine], -1)], axis=1
    )
    turned = np.stack([cosine.transpose(0, 2, 1), sine.transpose(0, 2, 1)], axis=1)
    return flat.astype(np.float32), turned.astype(np.float32)


def nt(a, b):
    return lax.dot_general(a, b, (((1,), (1,)), ((), ())), preferred_element_type=jnp.float32)


def tn(a, b):
    return lax.dot_general(a, b, (((0,), (0,)), ((), ())), preferred_element_type=jnp.float32)


def kernel(
    ctx,
    dps,
    parents,
    q_in,
    k_in,
    v_in,
    g_in,
    q_bias,
    k_bias,
    v_bias,
    flat_table,
    turned_table,
    att_out,
    dq_out,
    dk_out,
    dv_out,
    qb_out,
    kb_out,
    vb_out,
    negs,
    flat,
    turned,
    causal,
    kv,
    qt,
    gt,
    scores,
    low,
    acc,
    own,
    part,
    landed,
    totals,
    totals_ctx,
    totals_dp,
    kv_send,
    kv_recv,
    part_send,
    part_recv,
    ctx_send,
    ctx_recv,
    dp_send,
    dp_recv,
):
    head = pl.program_id(0)
    me = lax.axis_index("ctx")
    dp = lax.axis_index("dp")
    rows = k_in.shape[0]
    pairs = (me + 2) // 2

    def kv_copy(h, source, target):
        return pltpu.make_async_remote_copy(
            src_ref=kv.at[h, :, source],
            dst_ref=kv.at[h, :, source],
            send_sem=kv_send.at[h, target],
            recv_sem=kv_recv.at[h, source],
            device_id={"ctx": target},
            device_id_type=MESH,
        )

    def part_copy(h, sender, owner):
        return pltpu.make_async_remote_copy(
            src_ref=part.at[h, :, owner],
            dst_ref=landed.at[h, :, sender],
            send_sem=part_send.at[h, owner],
            recv_sem=part_recv.at[h, sender],
            device_id={"ctx": owner},
            device_id_type=MESH,
        )

    @pl.when(head == 0)
    def _():
        barrier = pltpu.get_barrier_semaphore()

        @pl.loop(1, ctx)
        def _(step):
            pl.semaphore_signal(
                barrier, inc=1, device_id={"ctx": lax.rem(me + step, ctx)}, device_id_type=MESH
            )

        @pl.loop(1, dps)
        def _(step):
            pl.semaphore_signal(
                barrier, inc=1, device_id={"dp": lax.rem(dp + step, dps)}, device_id_type=MESH
            )

        path = [me]
        depth = jnp.int32(0)
        for _ in range(ctx - 1):
            depth = depth + jnp.where(path[-1] != 0, 1, 0).astype(jnp.int32)
            path.append(parents[0, path[-1]])
        for block in range(ctx):
            seen = path[0] == block
            for node in path[1:]:
                seen = seen | (node == block)
            negs[block] = jnp.where(seen, jnp.float32(0.0), jnp.float32(NEG_LARGE))
        flat[...] = flat_table[depth]
        turned[...] = turned_table[depth]
        key_id = lax.broadcasted_iota(jnp.int32, (rows, rows), 0)
        row_id = lax.broadcasted_iota(jnp.int32, (rows, rows), 1)
        causal[...] = jnp.where(key_id <= row_id, 0.0, NEG_LARGE).astype(jnp.float32)
        for h in range(KV_HEADS):
            columns = pl.ds(h * HEAD, HEAD)
            x = k_in[:, columns].astype(jnp.float32) + k_bias[pl.ds(h, 1), :]
            x = x * flat[0] + pltpu.roll(x, HALF, 1) * flat[1]
            kv[h, 0, me] = x.astype(jnp.bfloat16)
            v = v_in[:, columns].astype(jnp.float32) + v_bias[pl.ds(h, 1), :]
            kv[h, 1, me] = v.astype(jnp.bfloat16)

        @pl.when(2 * pairs > me + 1)
        def _():
            for h in range(KV_HEADS):
                for which in range(2):
                    kv[h, which, me + 1] = jnp.zeros((rows, HEAD), jnp.bfloat16)

        pl.semaphore_wait(barrier, ctx + dps - 2)

        @pl.loop(0, KV_HEADS)
        def _(h):
            @pl.loop(0, ctx - 1 - me)
            def _(step):
                kv_copy(h, me, ctx - 1 - step).start()

    for g in range(GROUP):
        columns = pl.ds(g * HEAD, HEAD)
        x = (q_in[:, columns].astype(jnp.float32) + q_bias[pl.ds(g, 1), :]).T
        first, second = x[:HALF], x[HALF:]
        cosine, sine = turned[0] * LOG2_SCALE, turned[1] * LOG2_SCALE
        qt[pl.ds(0, HALF), columns] = (first * cosine - second * sine).astype(jnp.bfloat16)
        qt[pl.ds(HALF, HALF), columns] = (second * cosine + first * sine).astype(jnp.bfloat16)
        gt[:, columns] = g_in[:, columns].T

    @pl.loop(0, me)
    def _(source):
        kv_copy(head, source, me).wait_recv()

    def keys_of(which, pair):
        return kv[head, which, pl.ds(2 * pair, 2)].reshape(2 * rows, HEAD)

    wide = GROUP * rows

    def score_pair(pair, peak):
        tile = jnp.dot(keys_of(0, pair), qt[...], preferred_element_type=jnp.float32)
        for side in range(2):
            block = 2 * pair + side
            reach = jnp.where(block > me, NEG_LARGE, negs[jnp.minimum(block, ctx - 1)])
            mask = jnp.where(block == me, causal[...], reach)
            piece = tile[side * rows : (side + 1) * rows] + jnp.tile(mask, (1, GROUP))
            scores[pair, pl.ds(side * rows, rows), :] = piece
            peak = jnp.maximum(peak, jnp.max(piece, axis=0, keepdims=True))
        return peak

    peak = lax.fori_loop(
        0, pairs, score_pair, jnp.full((1, wide), NEG_LARGE, jnp.float32)
    )
    acc[...] = jnp.zeros_like(acc)

    def weigh_pair(pair, total):
        weights = jnp.exp2(scores[pair] - peak)
        rounded = weights.astype(jnp.bfloat16)
        low[pair] = rounded
        acc[...] += tn(keys_of(1, pair), rounded)
        return total + jnp.sum(weights, axis=0, keepdims=True)

    total = lax.fori_loop(0, pairs, weigh_pair, jnp.zeros((1, wide), jnp.float32))
    inverse = 1.0 / total
    attended = (acc[...] * inverse).astype(jnp.bfloat16)
    for g in range(GROUP):
        att_out[:, pl.ds(g * HEAD, HEAD)] = attended[:, g * HEAD : (g + 1) * HEAD].T
    grad = gt[...].astype(jnp.float32)
    delta = jnp.sum(grad * attended.astype(jnp.float32), axis=0, keepdims=True) * inverse
    gt[...] = (grad * inverse).astype(jnp.bfloat16)
    acc[...] = jnp.zeros_like(acc)

    @pl.loop(0, pairs)
    def _(pair):
        keys, values = keys_of(0, pair), keys_of(1, pair)
        rounded = low[pair]
        slopes = jnp.dot(values, gt[...], preferred_element_type=jnp.float32)
        steep = (rounded.astype(jnp.float32) * (slopes - delta)).astype(jnp.bfloat16)
        acc[...] += tn(keys, steep)
        key_part = nt(steep, qt[...]) * LN2
        value_part = nt(rounded, gt[...])
        for side in range(2):
            block = 2 * pair + side
            piece = slice(side * rows, (side + 1) * rows)

            @pl.when(block < me)
            def _():
                part[head, 0, block] = key_part[piece].astype(jnp.bfloat16)
                part[head, 1, block] = value_part[piece].astype(jnp.bfloat16)
                part_copy(head, me, block).start()

            @pl.when(block == me)
            def _():
                own[head, 0] = key_part[piece]
                own[head, 1] = value_part[piece]

    sums = []
    for g in range(GROUP):
        columns = pl.ds(g * HEAD, HEAD)
        x = acc[:, columns] * SCALE
        first, second = x[:HALF], x[HALF:]
        cosine, sine = turned[0], turned[1]
        back = jnp.concatenate(
            [first * cosine + second * sine, second * cosine - first * sine], axis=0
        ).T
        dq_out[:, columns] = back
        sums.append(jnp.sum(back, axis=0, keepdims=True))
    totals[pl.ds(pl.multiple_of(head * GROUP, GROUP), GROUP), :] = jnp.concatenate(sums, axis=0)

    @pl.when(head == KV_HEADS - 1)
    def _():
        for h in range(KV_HEADS):

            @pl.loop(me + 1, ctx)
            def _(sender):
                part_copy(h, sender, me).wait_recv()
                own[h] += landed[h, :, sender].astype(jnp.float32)

            x = own[h, 0]
            x = x * flat[0] - pltpu.roll(x, HALF, 1) * flat[1]
            columns = pl.ds(h * HEAD, HEAD)
            dk_out[:, columns] = x
            v = own[h, 1]
            dv_out[:, columns] = v
            totals[pl.ds(Q_HEADS + h, 1), :] = jnp.sum(x, axis=0, keepdims=True)
            totals[pl.ds(Q_HEADS + KV_HEADS + h, 1), :] = jnp.sum(v, axis=0, keepdims=True)

        def total_copy(axis, peer, slot, source, landing, send, recv):
            return pltpu.make_async_remote_copy(
                src_ref=source,
                dst_ref=landing.at[slot],
                send_sem=send.at[peer],
                recv_sem=recv.at[slot],
                device_id={axis: peer},
                device_id_type=MESH,
            )

        def exchange(axis, size, index, source, landing, send, recv):
            landing[index] = source[...]

            @pl.loop(1, size)
            def _(step):
                peer = lax.rem(index + step, size)
                total_copy(axis, peer, index, source, landing, send, recv).start()

            @pl.loop(1, size)
            def _(step):
                peer = lax.rem(index + step, size)
                total_copy(axis, peer, peer, source, landing, send, recv).wait_recv()

            result = landing[0]
            for slot in range(1, size):
                result = result + landing[slot]

            @pl.loop(1, size)
            def _(step):
                peer = lax.rem(index + step, size)
                total_copy(axis, peer, index, source, landing, send, recv).wait_send()

            return result

        totals[...] = exchange("ctx", ctx, me, totals, totals_ctx, ctx_send, ctx_recv)
        result = exchange("dp", dps, dp, totals, totals_dp, dp_send, dp_recv)
        qb_out[...] = result[:Q_HEADS]
        kb_out[...] = result[Q_HEADS : Q_HEADS + KV_HEADS]
        vb_out[...] = result[Q_HEADS + KV_HEADS :]

        @pl.loop(0, KV_HEADS)
        def _(h):
            @pl.loop(me + 1, ctx)
            def _(target):
                kv_copy(h, me, target).wait_send()

            @pl.loop(0, me)
            def _(owner):
                part_copy(h, me, owner).wait_send()


def body(query_input, key_input, value_input, out_grad, query_bias, key_bias, value_bias, parents):
    ctx, dps = lax.axis_size("ctx"), lax.axis_size("dp")
    _, rows, query_width = query_input.shape
    key_width = key_input.shape[2]
    flat_table, turned_table = tables(ctx, rows)
    f32, bf16 = jnp.float32, jnp.bfloat16
    whole = pl.BlockSpec(memory_space=pltpu.VMEM)
    wide = GROUP * rows
    group_block = pl.BlockSpec((rows, GROUP * HEAD), lambda h: (0, h))
    bias_rows = Q_HEADS + 2 * KV_HEADS
    dma = pltpu.SemaphoreType.DMA
    outs = pl.pallas_call(
        functools.partial(kernel, ctx, dps),
        grid=(KV_HEADS,),
        out_shape=(
            jax.ShapeDtypeStruct((rows, query_width), bf16),
            jax.ShapeDtypeStruct((rows, query_width), f32),
            jax.ShapeDtypeStruct((rows, key_width), f32),
            jax.ShapeDtypeStruct((rows, key_width), f32),
            jax.ShapeDtypeStruct((Q_HEADS, HEAD), f32),
            jax.ShapeDtypeStruct((KV_HEADS, HEAD), f32),
            jax.ShapeDtypeStruct((KV_HEADS, HEAD), f32),
        ),
        in_specs=[
            pl.BlockSpec(memory_space=pltpu.SMEM),
            group_block,
            whole,
            whole,
            group_block,
            pl.BlockSpec((GROUP, HEAD), lambda h: (h, 0)),
            whole,
            whole,
            whole,
            whole,
        ],
        out_specs=(group_block, group_block, whole, whole, whole, whole, whole),
        scratch_shapes=[
            pltpu.SMEM((ctx,), f32),
            pltpu.VMEM((2, rows, HEAD), f32),
            pltpu.VMEM((2, HALF, rows), f32),
            pltpu.VMEM((rows, rows), f32),
            pltpu.VMEM((KV_HEADS, 2, ctx, rows, HEAD), bf16),
            pltpu.VMEM((HEAD, wide), bf16),
            pltpu.VMEM((HEAD, wide), bf16),
            pltpu.VMEM((ctx // 2, 2 * rows, wide), f32),
            pltpu.VMEM((ctx // 2, 2 * rows, wide), bf16),
            pltpu.VMEM((HEAD, wide), f32),
            pltpu.VMEM((KV_HEADS, 2, rows, HEAD), f32),
            pltpu.VMEM((KV_HEADS, 2, ctx, rows, HEAD), bf16),
            pltpu.VMEM((KV_HEADS, 2, ctx, rows, HEAD), bf16),
            pltpu.VMEM((bias_rows, HEAD), f32),
            pltpu.VMEM((ctx, bias_rows, HEAD), f32),
            pltpu.VMEM((dps, bias_rows, HEAD), f32),
            dma((KV_HEADS, ctx)),
            dma((KV_HEADS, ctx)),
            dma((KV_HEADS, ctx)),
            dma((KV_HEADS, ctx)),
            dma((ctx,)),
            dma((ctx,)),
            dma((dps,)),
            dma((dps,)),
        ],
        compiler_params=pltpu.CompilerParams(
            collective_id=0,
            has_side_effects=True,
            vmem_limit_bytes=58 * 1024 * 1024,
            dimension_semantics=("arbitrary",),
        ),
    )(
        parents,
        query_input[0],
        key_input[0],
        value_input[0],
        out_grad[0],
        query_bias.reshape(Q_HEADS, HEAD),
        key_bias.reshape(KV_HEADS, HEAD),
        value_bias.reshape(KV_HEADS, HEAD),
        jnp.asarray(flat_table),
        jnp.asarray(turned_table),
    )
    attended, query_grad, key_grad, value_grad, query_total, key_total, value_total = outs
    return (
        attended[None],
        query_grad[None],
        key_grad[None],
        value_grad[None],
        query_total.reshape(-1),
        key_total.reshape(-1),
        value_total.reshape(-1),
    )


def solution(mesh):
    split = P("dp", "ctx", None)
    return jax.shard_map(
        body,
        mesh=mesh,
        in_specs=(split, split, split, split, P(), P(), P(), P("dp", None)),
        out_specs=(split, split, split, split, P(), P(), P()),
        check_vma=False,
    )
```

```python
import functools
import math

import jax
import jax.numpy as jnp
import numpy as np
from jax import lax
from jax.experimental import pallas as pl
from jax.experimental.pallas import tpu as pltpu
from jax.sharding import PartitionSpec as P

Q_HEADS = 64
KV_HEADS = 8
HEAD = 128
GROUP = Q_HEADS // KV_HEADS
HALF = HEAD // 2
NEG_LARGE = -1e30
SCALE = HEAD ** (-0.5)
LOG2_SCALE = SCALE * math.log2(math.e)
LN2 = math.log(2.0)
MESH = pl.DeviceIdType.MESH


def tables(depths, rows):
    frequency = 1000000.0 ** (-2.0 * np.arange(HALF) / HEAD)
    places = (np.arange(depths)[:, None] * rows + np.arange(rows)[None, :]).astype(np.float64)
    angles = places[..., None] * frequency
    cosine, sine = np.cos(angles), np.sin(angles)
    flat = np.stack(
        [np.concatenate([cosine, cosine], -1), np.concatenate([-sine, sine], -1)], axis=1
    )
    turned = np.stack([cosine.transpose(0, 2, 1), sine.transpose(0, 2, 1)], axis=1)
    return flat.astype(np.float32), turned.astype(np.float32)


def nt(a, b):
    return lax.dot_general(a, b, (((1,), (1,)), ((), ())), preferred_element_type=jnp.float32)


def tn(a, b):
    return lax.dot_general(a, b, (((0,), (0,)), ((), ())), preferred_element_type=jnp.float32)


def kernel(
    ctx,
    dps,
    parents,
    q_in,
    k_in,
    v_in,
    g_in,
    q_bias,
    k_bias,
    v_bias,
    flat_table,
    turned_table,
    att_out,
    dq_out,
    dk_out,
    dv_out,
    qb_out,
    kb_out,
    vb_out,
    negs,
    flat,
    turned,
    causal,
    kv,
    qt,
    gt,
    scores,
    low,
    acc,
    own,
    part,
    pool,
    landed,
    totals,
    totals_ctx,
    totals_dp,
    kv_send,
    kv_recv,
    relay_send,
    part_send,
    pool_recv,
    part_recv,
    ctx_send,
    ctx_recv,
    dp_send,
    dp_recv,
):
    head = pl.program_id(0)
    me = lax.axis_index("ctx")
    dp = lax.axis_index("dp")
    rows = k_in.shape[0]
    pairs = (me + 2) // 2

    chips = ctx // 2
    chip, side_of = me // 2, lax.rem(me, 2)
    sibling = me + 1 - 2 * side_of

    def kv_copy(h, source, target, send_sem):
        return pltpu.make_async_remote_copy(
            src_ref=kv.at[h, :, source],
            dst_ref=kv.at[h, :, source],
            send_sem=send_sem,
            recv_sem=kv_recv.at[h, source],
            device_id={"ctx": target},
            device_id_type=MESH,
        )

    def own_copy(h, target):
        return kv_copy(h, me, target, kv_send.at[h, target])

    def relay_copy(h, source):
        return kv_copy(h, source, sibling, relay_send.at[h, source])

    def relay(h):
        @pl.loop(0, chip)
        def _(other):
            source = 2 * other + side_of
            relay_copy(h, source).wait_recv()
            relay_copy(h, source).start()

    def pool_copy(h, block):
        return pltpu.make_async_remote_copy(
            src_ref=part.at[h, :, block],
            dst_ref=pool.at[h, :, block // 2],
            send_sem=part_send.at[h, block],
            recv_sem=pool_recv.at[h, block // 2],
            device_id={"ctx": sibling},
            device_id_type=MESH,
        )

    def part_copy(h, sender, owner):
        return pltpu.make_async_remote_copy(
            src_ref=part.at[h, :, owner],
            dst_ref=landed.at[h, :, sender],
            send_sem=part_send.at[h, owner],
            recv_sem=part_recv.at[h, sender],
            device_id={"ctx": owner},
            device_id_type=MESH,
        )

    def combine(h):
        @pl.loop(0, chip)
        def _(other):
            owner = 2 * other + side_of
            pool_copy(h, owner).wait_recv()
            summed = part[h, :, owner].astype(jnp.float32) + pool[h, :, other].astype(jnp.float32)
            part[h, :, owner] = summed.astype(jnp.bfloat16)
            part_copy(h, chip, owner).start()

        @pl.when(side_of == 0)
        def _():
            pool_copy(h, me).wait_recv()
            own[h] += pool[h, :, chip].astype(jnp.float32)

    @pl.when(head == 0)
    def _():
        barrier = pltpu.get_barrier_semaphore()

        @pl.loop(1, ctx)
        def _(step):
            pl.semaphore_signal(
                barrier, inc=1, device_id={"ctx": lax.rem(me + step, ctx)}, device_id_type=MESH
            )

        @pl.loop(1, dps)
        def _(step):
            pl.semaphore_signal(
                barrier, inc=1, device_id={"dp": lax.rem(dp + step, dps)}, device_id_type=MESH
            )

        path = [me]
        depth = jnp.int32(0)
        for _ in range(ctx - 1):
            depth = depth + jnp.where(path[-1] != 0, 1, 0).astype(jnp.int32)
            path.append(parents[0, path[-1]])
        for block in range(ctx):
            seen = path[0] == block
            for node in path[1:]:
                seen = seen | (node == block)
            negs[block] = jnp.where(seen, jnp.float32(0.0), jnp.float32(NEG_LARGE))
        flat[...] = flat_table[depth]
        turned[...] = turned_table[depth]
        key_id = lax.broadcasted_iota(jnp.int32, (rows, rows), 0)
        row_id = lax.broadcasted_iota(jnp.int32, (rows, rows), 1)
        causal[...] = jnp.where(key_id <= row_id, 0.0, NEG_LARGE).astype(jnp.float32)
        for h in range(KV_HEADS):
            columns = pl.ds(h * HEAD, HEAD)
            x = k_in[:, columns].astype(jnp.float32) + k_bias[pl.ds(h, 1), :]
            x = x * flat[0] + pltpu.roll(x, HALF, 1) * flat[1]
            kv[h, 0, me] = x.astype(jnp.bfloat16)
            v = v_in[:, columns].astype(jnp.float32) + v_bias[pl.ds(h, 1), :]
            kv[h, 1, me] = v.astype(jnp.bfloat16)

        @pl.when(2 * pairs > me + 1)
        def _():
            for h in range(KV_HEADS):
                for which in range(2):
                    kv[h, which, me + 1] = jnp.zeros((rows, HEAD), jnp.bfloat16)

        pl.semaphore_wait(barrier, ctx + dps - 2)

        @pl.loop(0, KV_HEADS)
        def _(h):
            @pl.when(side_of == 0)
            def _():
                own_copy(h, sibling).start()

            @pl.loop(0, chips - 1 - chip)
            def _(step):
                own_copy(h, 2 * (chips - 1 - step) + side_of).start()

        relay(0)

    for g in range(GROUP):
        columns = pl.ds(g * HEAD, HEAD)
        x = (q_in[:, columns].astype(jnp.float32) + q_bias[pl.ds(g, 1), :]).T
        first, second = x[:HALF], x[HALF:]
        cosine, sine = turned[0] * LOG2_SCALE, turned[1] * LOG2_SCALE
        qt[pl.ds(0, HALF), columns] = (first * cosine - second * sine).astype(jnp.bfloat16)
        qt[pl.ds(HALF, HALF), columns] = (second * cosine + first * sine).astype(jnp.bfloat16)
        gt[:, columns] = g_in[:, columns].T

    @pl.loop(0, chip + side_of)
    def _(other):
        source = 2 * other + 1 - side_of
        relay_copy(head, source).wait_recv()

    def keys_of(which, pair):
        return kv[head, which, pl.ds(2 * pair, 2)].reshape(2 * rows, HEAD)

    wide = GROUP * rows

    def score_pair(pair, peak):
        tile = jnp.dot(keys_of(0, pair), qt[...], preferred_element_type=jnp.float32)
        for side in range(2):
            block = 2 * pair + side
            reach = jnp.where(block > me, NEG_LARGE, negs[jnp.minimum(block, ctx - 1)])
            mask = jnp.where(block == me, causal[...], reach)
            piece = tile[side * rows : (side + 1) * rows] + jnp.tile(mask, (1, GROUP))
            scores[pair, pl.ds(side * rows, rows), :] = piece
            peak = jnp.maximum(peak, jnp.max(piece, axis=0, keepdims=True))
        return peak

    peak = lax.fori_loop(
        0, pairs, score_pair, jnp.full((1, wide), NEG_LARGE, jnp.float32)
    )
    acc[...] = jnp.zeros_like(acc)

    @pl.when(head < KV_HEADS - 1)
    def _():
        relay(head + 1)

    @pl.when(head > 0)
    def _():
        combine(head - 1)

    def weigh_pair(pair, total):
        weights = jnp.exp2(scores[pair] - peak)
        rounded = weights.astype(jnp.bfloat16)
        low[pair] = rounded
        acc[...] += tn(keys_of(1, pair), rounded)
        return total + jnp.sum(weights, axis=0, keepdims=True)

    total = lax.fori_loop(0, pairs, weigh_pair, jnp.zeros((1, wide), jnp.float32))
    inverse = 1.0 / total
    attended = (acc[...] * inverse).astype(jnp.bfloat16)
    for g in range(GROUP):
        att_out[:, pl.ds(g * HEAD, HEAD)] = attended[:, g * HEAD : (g + 1) * HEAD].T
    grad = gt[...].astype(jnp.float32)
    delta = jnp.sum(grad * attended.astype(jnp.float32), axis=0, keepdims=True) * inverse
    gt[...] = (grad * inverse).astype(jnp.bfloat16)
    acc[...] = jnp.zeros_like(acc)

    @pl.loop(0, pairs)
    def _(pair):
        keys, values = keys_of(0, pair), keys_of(1, pair)
        rounded = low[pair]
        slopes = jnp.dot(values, gt[...], preferred_element_type=jnp.float32)
        steep = (rounded.astype(jnp.float32) * (slopes - delta)).astype(jnp.bfloat16)
        acc[...] += tn(keys, steep)
        key_part = nt(steep, qt[...]) * LN2
        value_part = nt(rounded, gt[...])
        for side in range(2):
            block = 2 * pair + side
            piece = slice(side * rows, (side + 1) * rows)

            @pl.when(block < me)
            def _():
                part[head, 0, block] = key_part[piece].astype(jnp.bfloat16)
                part[head, 1, block] = value_part[piece].astype(jnp.bfloat16)

            @pl.when((block < me) & (side != side_of))
            def _():
                pool_copy(head, block).start()

            @pl.when(block == me)
            def _():
                own[head, 0] = key_part[piece]
                own[head, 1] = value_part[piece]

    sums = []
    for g in range(GROUP):
        columns = pl.ds(g * HEAD, HEAD)
        x = acc[:, columns] * SCALE
        first, second = x[:HALF], x[HALF:]
        cosine, sine = turned[0], turned[1]
        back = jnp.concatenate(
            [first * cosine + second * sine, second * cosine - first * sine], axis=0
        ).T
        dq_out[:, columns] = back
        sums.append(jnp.sum(back, axis=0, keepdims=True))
    totals[pl.ds(pl.multiple_of(head * GROUP, GROUP), GROUP), :] = jnp.concatenate(sums, axis=0)

    @pl.when(head == KV_HEADS - 1)
    def _():
        combine(KV_HEADS - 1)
        for h in range(KV_HEADS):

            @pl.loop(chip + 1, chips)
            def _(sender):
                part_copy(h, sender, me).wait_recv()
                own[h] += landed[h, :, sender].astype(jnp.float32)

            x = own[h, 0]
            x = x * flat[0] - pltpu.roll(x, HALF, 1) * flat[1]
            columns = pl.ds(h * HEAD, HEAD)
            dk_out[:, columns] = x
            v = own[h, 1]
            dv_out[:, columns] = v
            totals[pl.ds(Q_HEADS + h, 1), :] = jnp.sum(x, axis=0, keepdims=True)
            totals[pl.ds(Q_HEADS + KV_HEADS + h, 1), :] = jnp.sum(v, axis=0, keepdims=True)

        def total_copy(axis, peer, slot, source, landing, send, recv):
            return pltpu.make_async_remote_copy(
                src_ref=source,
                dst_ref=landing.at[slot],
                send_sem=send.at[peer],
                recv_sem=recv.at[slot],
                device_id={axis: peer},
                device_id_type=MESH,
            )

        def exchange(axis, size, index, source, landing, send, recv):
            landing[index] = source[...]

            @pl.loop(1, size)
            def _(step):
                peer = lax.rem(index + step, size)
                total_copy(axis, peer, index, source, landing, send, recv).start()

            @pl.loop(1, size)
            def _(step):
                peer = lax.rem(index + step, size)
                total_copy(axis, peer, peer, source, landing, send, recv).wait_recv()

            result = landing[0]
            for slot in range(1, size):
                result = result + landing[slot]

            @pl.loop(1, size)
            def _(step):
                peer = lax.rem(index + step, size)
                total_copy(axis, peer, index, source, landing, send, recv).wait_send()

            return result

        totals[...] = exchange("ctx", ctx, me, totals, totals_ctx, ctx_send, ctx_recv)
        result = exchange("dp", dps, dp, totals, totals_dp, dp_send, dp_recv)
        qb_out[...] = result[:Q_HEADS]
        kb_out[...] = result[Q_HEADS : Q_HEADS + KV_HEADS]
        vb_out[...] = result[Q_HEADS + KV_HEADS :]

        @pl.loop(0, KV_HEADS)
        def _(h):
            @pl.when(side_of == 0)
            def _():
                own_copy(h, sibling).wait_send()

            @pl.loop(chip + 1, chips)
            def _(target):
                own_copy(h, 2 * target + side_of).wait_send()

            @pl.loop(0, chip)
            def _(other):
                relay_copy(h, 2 * other + side_of).wait_send()

            @pl.loop(0, me)
            def _(owner):
                pool_copy(h, owner).wait_send()


def body(query_input, key_input, value_input, out_grad, query_bias, key_bias, value_bias, parents):
    ctx, dps = lax.axis_size("ctx"), lax.axis_size("dp")
    _, rows, query_width = query_input.shape
    key_width = key_input.shape[2]
    flat_table, turned_table = tables(ctx, rows)
    f32, bf16 = jnp.float32, jnp.bfloat16
    whole = pl.BlockSpec(memory_space=pltpu.VMEM)
    wide = GROUP * rows
    group_block = pl.BlockSpec((rows, GROUP * HEAD), lambda h: (0, h))
    bias_rows = Q_HEADS + 2 * KV_HEADS
    dma = pltpu.SemaphoreType.DMA
    outs = pl.pallas_call(
        functools.partial(kernel, ctx, dps),
        grid=(KV_HEADS,),
        out_shape=(
            jax.ShapeDtypeStruct((rows, query_width), bf16),
            jax.ShapeDtypeStruct((rows, query_width), f32),
            jax.ShapeDtypeStruct((rows, key_width), f32),
            jax.ShapeDtypeStruct((rows, key_width), f32),
            jax.ShapeDtypeStruct((Q_HEADS, HEAD), f32),
            jax.ShapeDtypeStruct((KV_HEADS, HEAD), f32),
            jax.ShapeDtypeStruct((KV_HEADS, HEAD), f32),
        ),
        in_specs=[
            pl.BlockSpec(memory_space=pltpu.SMEM),
            group_block,
            whole,
            whole,
            group_block,
            pl.BlockSpec((GROUP, HEAD), lambda h: (h, 0)),
            whole,
            whole,
            whole,
            whole,
        ],
        out_specs=(group_block, group_block, whole, whole, whole, whole, whole),
        scratch_shapes=[
            pltpu.SMEM((ctx,), f32),
            pltpu.VMEM((2, rows, HEAD), f32),
            pltpu.VMEM((2, HALF, rows), f32),
            pltpu.VMEM((rows, rows), f32),
            pltpu.VMEM((KV_HEADS, 2, ctx, rows, HEAD), bf16),
            pltpu.VMEM((HEAD, wide), bf16),
            pltpu.VMEM((HEAD, wide), bf16),
            pltpu.VMEM((ctx // 2, 2 * rows, wide), f32),
            pltpu.VMEM((ctx // 2, 2 * rows, wide), bf16),
            pltpu.VMEM((HEAD, wide), f32),
            pltpu.VMEM((KV_HEADS, 2, rows, HEAD), f32),
            pltpu.VMEM((KV_HEADS, 2, ctx, rows, HEAD), bf16),
            pltpu.VMEM((KV_HEADS, 2, ctx // 2, rows, HEAD), bf16),
            pltpu.VMEM((KV_HEADS, 2, ctx // 2, rows, HEAD), bf16),
            pltpu.VMEM((bias_rows, HEAD), f32),
            pltpu.VMEM((ctx, bias_rows, HEAD), f32),
            pltpu.VMEM((dps, bias_rows, HEAD), f32),
            dma((KV_HEADS, ctx)),
            dma((KV_HEADS, ctx)),
            dma((KV_HEADS, ctx)),
            dma((KV_HEADS, ctx)),
            dma((KV_HEADS, ctx // 2)),
            dma((KV_HEADS, ctx // 2)),
            dma((ctx,)),
            dma((ctx,)),
            dma((dps,)),
            dma((dps,)),
        ],
        compiler_params=pltpu.CompilerParams(
            collective_id=0,
            has_side_effects=True,
            vmem_limit_bytes=58 * 1024 * 1024,
            dimension_semantics=("arbitrary",),
        ),
    )(
        parents,
        query_input[0],
        key_input[0],
        value_input[0],
        out_grad[0],
        query_bias.reshape(Q_HEADS, HEAD),
        key_bias.reshape(KV_HEADS, HEAD),
        value_bias.reshape(KV_HEADS, HEAD),
        jnp.asarray(flat_table),
        jnp.asarray(turned_table),
    )
    attended, query_grad, key_grad, value_grad, query_total, key_total, value_total = outs
    return (
        attended[None],
        query_grad[None],
        key_grad[None],
        value_grad[None],
        query_total.reshape(-1),
        key_total.reshape(-1),
        value_total.reshape(-1),
    )


def solution(mesh):
    split = P("dp", "ctx", None)
    return jax.shard_map(
        body,
        mesh=mesh,
        in_specs=(split, split, split, split, P(), P(), P(), P("dp", None)),
        out_specs=(split, split, split, split, P(), P(), P()),
        check_vma=False,
    )
```
